128 devices in a mesh: ind: 8 (over z_hi, y), var: 16 (over z_lo, x, core).
Axes of the slice: x: 4, y: 4, z: 4 (z_hi: 2, z_lo: 2; z = z_hi * 2 + z_lo), core: 2. Of those that a mesh axis runs over, the one named last changes fastest.
Arguments:
- genotypes: bfloat16 [2048, 786432], P('var', 'ind'), may hold values from -6 to 6, as said below
- residual: float32 [786432], P('ind'), may hold values from -6 to 6
- ancestry: int32 [786432], P('ind'), may hold values from 0 to 4, never falling along the last dimension, each value on 1 to 393216 neighbouring positions
- effects: float32 [5, 2048], P(None, 'var'), may hold values from -4 to 4
- prior_precision: float32 [5, 5], replicated, may hold values from -12 to 12, as said below
- noise_var: float32 [5], replicated, may hold values from 0.5 to 2
- block_index: int32 [3, 512], P(None, 'var'), may hold values from 0 to 127, as said below
- gaussians: float32 [3, 5, 512], P(None, None, 'var'), may hold values from -5 to 5
Outputs:
- new_residual: float32 [786432], P(('ind', 'var'))
- new_effects: float32 [5, 2048], P(None, 'var')
The draws below stay inside these ranges and needn't reach their ends.
Inputs may be any that keep to these rules, and one draw needn't show every extreme that they name: Scaled genotypes; variants and individuals have different scales. `prior_precision`: symmetric positive definite. `block_index`: in each step the 32 entries held by one index of var are distinct rows among that index's 128 variants; rows 0 and 127 appear in every draw.
All inputs are finite; a program needn't handle non-finite values.
Results may differ from the reference program's by a relative error of at most 0.0003.
Values sent between devices are 32-bit elements; how exact they have to be, the bound alone decides.
A program may use at most 128 MiB of HBM per device.

```python
import math
import jax
import jax.numpy as jnp
import numpy as np
from jax import lax

K = 5
COLS = 128
BV = 32
STEPS = 3
NI = 786432
M = 2048
BLOCK = 512
N_VAR = 16


def draw_genotypes(key, part):
    col_key = jax.random.fold_in(key, 11)
    row_key = jax.random.fold_in(key, 12)
    base_key = jax.random.fold_in(key, 13)
    col_scale = jnp.exp(jax.random.uniform(col_key, (M, 1), jnp.float32, jnp.log(0.3), jnp.log(3.0)))
    row_scale = jnp.exp(jax.random.uniform(row_key, (1, NI), jnp.float32, jnp.log(0.3), jnp.log(3.0)))
    base = jnp.clip(jax.random.normal(base_key, (M, NI), jnp.float32), -4.0, 4.0)
    values = col_scale * row_scale * base / jnp.sqrt(jnp.float32(NI / K))
    return values.astype(jnp.bfloat16)


def draw_prior_precision(key, part):
    inner_key = jax.random.fold_in(key, 21)
    factor = 0.6 * jnp.clip(jax.random.normal(inner_key, (K, K), jnp.float32), -2.5, 2.5)
    return 0.5 * jnp.eye(K, dtype=jnp.float32) + jnp.dot(factor, factor.T)


def draw_block_index(key, part):
    groups = BLOCK // BV
    order_key = jax.random.fold_in(key, 31)
    column = jnp.arange(COLS, dtype=jnp.int32)
    ranking = jax.random.randint(order_key, (STEPS, groups, COLS), 0, 1 << 20, dtype=jnp.int32) * COLS + column
    first = (jnp.arange(STEPS)[:, None, None] == 0) & (jnp.arange(groups)[None, :, None] == 0)
    ends = (column == 0) | (column == COLS - 1)
    ranking = jnp.where(first & ends[None, None, :], -1 - column, ranking)
    order = jnp.argsort(ranking, axis=2, stable=True)[:, :, :BV]
    return order.reshape(STEPS, BLOCK).astype(jnp.int32)


def level_of(stream_key, extent, cuts, smallest, largest):
    level, own = 1.0, jax.random.fold_in(stream_key, 6)
    for axis_at, blocks in cuts:
        heights = jnp.exp(jax.random.uniform(jax.random.fold_in(own, axis_at), (blocks,), jnp.float32, smallest / len(cuts), largest / len(cuts)))
        level = level * jnp.repeat(heights, extent[axis_at] // blocks).reshape([-1 if axis == axis_at else 1 for axis in range(len(extent))])
    return level


def length_profile(number_of, total, limit, skew):
    weights = [(1 << 20) // math.isqrt(grade ** skew) + 1 for grade in range(2, number_of + 1)]
    rest, counts = total - limit - (number_of - 1), [1] * (number_of - 1)
    while rest > 0:
        candidates = [i for i in range(number_of - 1) if counts[i] < limit]
        mass, left = sum([weights[i] for i in candidates]), rest
        for i in candidates:
            addition = min(limit - counts[i], max(1, left * weights[i] // mass), rest)
            counts[i] = counts[i] + addition
            rest = rest - addition
    return np.array([limit] + counts)


def ragged(own_key, count, total, most, lean):
    if count == 2:
        one = jax.random.randint(own_key, (), max(1, total - most), min(most, total - 1) + 1)
        return jnp.stack([one, total - one])
    sizes = jnp.asarray(length_profile(count, total, most, lean), jnp.int32)
    pairs = (count - 1) // 2
    giver, sink = sizes[1:1 + 2 * pairs:2], sizes[2:2 + 2 * pairs:2]
    slack = jnp.minimum(giver - 1, most - sink)
    moved = jax.random.randint(jax.random.fold_in(own_key, 1), (pairs,), 0, 1 << 20) % (slack + 1)
    sizes = sizes.at[1:1 + 2 * pairs:2].set(giver - moved).at[2:2 + 2 * pairs:2].set(sink + moved)
    return sizes[jax.random.permutation(jax.random.fold_in(own_key, 2), count)]


def scatter_about(key, extent, scale, reach, cuts=(), kind=jnp.bfloat16):
    factor_of = level_of(key, extent, cuts, -0.22, 0.18) if cuts else 1.0
    result = jax.random.normal(key, extent, jnp.float32) * scale * factor_of
    return jnp.minimum(jnp.maximum(result, -reach), reach).astype(kind)


def setup_inputs(seed: int = 0) -> dict:
    key_list = jax.random.split(jax.random.key(seed), 9)
    genotypes = draw_genotypes(jax.random.fold_in(key_list[8], 71), 0)
    residual = scatter_about(key_list[1], (NI,), 1.0, 6.0, ((0, 8),), jnp.float32)
    ancestry = jnp.searchsorted(jnp.cumsum(ragged(key_list[2], K, NI, NI // 2, 2)), jnp.arange(NI), side="right").astype(jnp.int32)
    effects = scatter_about(key_list[3], (K, M), 0.5, 4.0, ((1, 16),), jnp.float32)
    prior_precision = draw_prior_precision(jax.random.fold_in(key_list[8], 71), 0)
    noise_var = jnp.clip(jnp.exp(jax.random.uniform(key_list[5], (K,), jnp.float32, math.log(0.5), math.log(2.0))), 0.5, 2.0)
    block_index = draw_block_index(jax.random.fold_in(key_list[8], 71), 0)
    gaussians = scatter_about(key_list[7], (STEPS, K, BLOCK), 1.0, 5.0, ((2, 16),), jnp.float32)
    return {"genotypes": genotypes, "residual": residual, "ancestry": ancestry, "effects": effects, "prior_precision": prior_precision, "noise_var": noise_var, "block_index": block_index, "gaussians": gaussians}


highest = lax.Precision.HIGHEST

def posterior_draw(scores, norm_sum, before, prior_precision, noise_var, noise_now):
    ancestries = scores.shape[0]
    inverse = 1.0 / noise_var
    target = (scores + norm_sum * before) * inverse[:, None]
    lower = [[None] * ancestries for column in range(ancestries)]
    for a in range(ancestries):
        for b in range(a + 1):
            total = prior_precision[a, b] + jnp.zeros_like(scores[0])
            if a == b:
                total = total + norm_sum[a] * inverse[a]
            for m in range(b):
                total = total - lower[a][m] * lower[b][m]
            if a == b:
                lower[a][a] = jnp.sqrt(total)
            else:
                lower[a][b] = total / lower[b][b]
    forward = []
    for a in range(ancestries):
        total = target[a]
        for m in range(a):
            total = total - lower[a][m] * forward[m]
        forward.append(total / lower[a][a] + noise_now[a])
    backward = [None] * ancestries
    for a in reversed(range(ancestries)):
        total = forward[a]
        for m in range(a + 1, ancestries):
            total = total - lower[m][a] * backward[m]
        backward[a] = total / lower[a][a]
    return jnp.stack(backward)

def reference(genotypes, residual, ancestry, effects, prior_precision, noise_var, block_index, gaussians):
    ancestries = effects.shape[0]
    onehot = (ancestry[None, :] == jnp.arange(ancestries, dtype=jnp.int32)[:, None]).astype(jnp.float32)
    offsets = (jnp.arange(BLOCK, dtype=jnp.int32) // BV * COLS).astype(jnp.int32)
    contract = (((1,), (1,)), ((), ()))
    for s in range(STEPS):
        picked = (block_index[s] + offsets).astype(jnp.int32)
        groups = picked.reshape(N_VAR, BV)
        weighted = onehot * residual[None, :]

        def score_group(indices):
            chosen = jnp.take(genotypes, indices, axis=0).astype(jnp.float32)
            first = lax.dot_general(weighted, chosen, contract, precision=highest)
            second = lax.dot_general(onehot, chosen * chosen, contract, precision=highest)
            return (first, second)
        scores, norm_sum = lax.map(score_group, groups)
        scores = scores.transpose(1, 0, 2).reshape(ancestries, BLOCK)
        norm_sum = norm_sum.transpose(1, 0, 2).reshape(ancestries, BLOCK)
        before = effects[:, picked]
        drawn = posterior_draw(scores, norm_sum, before, prior_precision, noise_var, gaussians[s])
        change = drawn - before
        effects = effects.at[:, picked].set(drawn)
        change_groups = change.reshape(ancestries, N_VAR, BV).transpose(1, 0, 2)

        def add_group(total, inputs):
            indices, delta = inputs
            chosen = jnp.take(genotypes, indices, axis=0).astype(jnp.float32)
            return (total + jnp.dot(delta, chosen, precision=highest), None)
        spread, unused = lax.scan(add_group, jnp.zeros((ancestries, NI), jnp.float32), (groups, change_groups))
        residual = residual - lax.optimization_barrier(jnp.sum(onehot * spread, axis=0))
    return (residual, effects)
```

```python
import functools

import jax
import jax.numpy as jnp
from jax import lax
from jax.experimental import pallas as pl
from jax.experimental.pallas import tpu as pltpu
from jax.sharding import PartitionSpec as P

MESH = pl.DeviceIdType.MESH
HIGHEST = lax.Precision.HIGHEST
F32 = jnp.float32

K = 5
ROWS = 128
BV = 32
STEPS = 3
NJ = 96
TJ = 6
NS = NJ // TJ
CJ = 3
NCH = NJ // CJ
NBUF = 6
N_IND = 8
FAR_FIRST = (6, 2, 5, 7, 4, 1, 3)
NEAR_FIRST = (1, 3, 4, 5, 7, 2, 6)


def far_first(m):
    return (2 + 3 * m + 3 * (m * (m - 1) // 2)) % 4


def kernel(
    g_hbm, r_hbm, places, eff_in, prior, noise, rows, rows_v, gauss,
    out_r, out_eff,
    wide, stage, r, eff, prefix, norm_prefix, part, spots, table, fix,
    norm_part, norm_span, factors, changes,
    core_send, core_recv, far_send, far_recv, norm_recv, ind_recv,
    load_sem, in_sem, core_ss, core_rs, far_ss, far_rs, ag_ss, ag_rs, fw_ss, fw_rs, nrm_ss, nrm_rs, ind_ss, ind_rs,
):
    ind, var = lax.axis_index("ind"), lax.axis_index("var")
    core, chip = var % 2, var // 2
    x, z = chip % 4, chip // 4
    y, zh = ind % 4, ind // 4
    partner = var + 1 - 2 * core

    def chip_at(o, sign):
        return ((z + o // 4) % 2) * 4 + (x + sign * (o % 4) + 4) % 4

    def ind_at(o):
        return ((zh + o // 4) % 2) * 4 + (y + o % 4) % 4

    def slice_tiles(w):
        return pl.ds(w * TJ, TJ)

    def remote(src, dst, send, recv, to):
        return pltpu.make_async_remote_copy(
            src_ref=src, dst_ref=dst, send_sem=send, recv_sem=recv, device_id=to, device_id_type=MESH
        )

    def chunk(c, slot):
        at = pl.multiple_of(c * CJ * 1024, CJ * 1024)
        return pltpu.make_async_copy(g_hbm.at[:, pl.ds(at, CJ * 1024)], stage.at[slot], load_sem.at[slot])

    def core_copy(o):
        return remote(core_send.at[o], core_recv.at[o], core_ss.at[o], core_rs.at[o], (ind, partner))

    def far_copy(o):
        return remote(
            far_send.at[o], far_recv.at[o], far_ss.at[o], far_rs.at[o], (ind, chip_at(o, 1) * 2 + core)
        )

    def gather_copy(o):
        own = slice_tiles(var)
        return remote(r.at[own], r.at[own], ag_ss.at[o], ag_rs.at[o], (ind, chip_at(o, 1) * 2 + core))

    def forward_copy(o):
        at = slice_tiles(chip_at(o, -1) * 2 + core)
        return remote(r.at[at], r.at[at], fw_ss.at[o], fw_rs.at[o], (ind, partner))

    def norm_copy(o):
        return remote(norm_recv.at[ind], norm_recv.at[ind], nrm_ss.at[o], nrm_rs.at[o], (ind_at(o), var))

    def ind_copy(s, o):
        return remote(ind_recv.at[s, ind], ind_recv.at[s, ind], ind_ss.at[s, o], ind_rs.at[s, o], (ind_at(o), var))

    r_copy = pltpu.make_async_copy(r_hbm, r, in_sem)
    r_copy.start()
    for c in range(NBUF):
        chunk(c, c).start()

    barrier = pltpu.get_barrier_semaphore()
    pl.semaphore_signal(barrier, inc=1, device_id=(ind, partner), device_id_type=MESH)
    for o in range(1, 8):
        pl.semaphore_signal(barrier, inc=1, device_id=(ind, chip_at(o, 1) * 2 + core), device_id_type=MESH)
    for o in range(1, N_IND):
        pl.semaphore_signal(barrier, inc=1, device_id=(ind_at(o), var), device_id_type=MESH)

    r_copy.wait()
    eff[...] = jnp.zeros_like(eff)
    eff[0:K, :] = eff_in[...]

    lanes = lax.broadcasted_iota(jnp.int32, (8, 128), 1)
    place = lax.broadcasted_iota(jnp.int32, (8, 128), 0) * 128 + lanes

    wide_rows = wide.reshape(NJ * ROWS * 8, 128)

    def tile(j, row):
        return wide[j * ROWS + row]

    def score_slice(s, q):
        held = [r[q * TJ + t] for t in range(TJ)]
        for c in range(BV):
            row = rows[s, c]
            total = prefix[q, c]
            for t in range(TJ):
                total = total + held[t] * tile(q * TJ + t, row)
            prefix[q + 1, c] = total

    prefix[0] = jnp.zeros_like(prefix[0])

    def load(q, norm):
        for h in range(TJ // CJ):
            c = q * (TJ // CJ) + h
            slot = lax.rem(c, NBUF)
            chunk(c, slot).wait()
            norm_prefix[c] = norm

            def widen(jj, norm):
                sums = [norm[a * 16 : (a + 1) * 16] for a in range(8)]
                for t in range(8):
                    at = pl.multiple_of(jj * 1024 + t * 128, 128)
                    for a in range(8):
                        v = stage[slot, a * 16 : (a + 1) * 16, pl.ds(at, 128)].astype(F32)
                        wide_rows[pl.ds((c * CJ + jj) * (ROWS * 8) + a * 128 + t, 16, stride=8), :] = v
                        sums[a] = sums[a] + v * v
                return jnp.concatenate(sums, axis=0)

            norm = lax.fori_loop(0, CJ, widen, norm)

            @pl.when(c + NBUF < NCH)
            def _():
                chunk(c + NBUF, slot).start()

        score_slice(0, q)
        return norm

    norm_all = lax.fori_loop(0, NS, load, jnp.zeros((ROWS, 128), F32))

    def pick_row(k, width):
        return (lax.broadcasted_iota(jnp.int32, (8, width), 0) == k).astype(F32)

    contract_last = (((1,), (1,)), ((), ()))

    def lane_sums(values):
        total = jnp.zeros((8, values[0].shape[0]), F32)
        for k in range(K):
            total = total + lax.dot_general(
                pick_row(k, 128), values[k], contract_last, precision=HIGHEST, preferred_element_type=F32
            )
        return total

    norm_span[K - 1] = jnp.zeros((ROWS, 128), F32)

    def norm_below(b, carry):
        c = places[16 + b]
        p = places[20 + b]
        keep = [t * 1024 + place < p for t in range(CJ)]

        def some_rows(a, carry):
            for i in range(8):
                total = jnp.zeros((8, 128), F32)
                for t in range(CJ):
                    v = tile(c * CJ + t, a * 8 + i)
                    total = total + jnp.where(keep[t], v * v, 0.0)
                norm_part[i * 8 : (i + 1) * 8, :] = total
            at = pl.ds(pl.multiple_of(a * 8, 8), 8)
            here = norm_prefix[c, at, :]
            for sub in range(8):
                here = here + norm_part[pl.ds(sub, 8, stride=8), :]
            norm_span[b, at, :] = here - norm_span[K - 1, at, :]
            norm_span[K - 1, at, :] = here
            return carry

        return lax.fori_loop(0, ROWS // 8, some_rows, carry)

    lax.fori_loop(0, K - 1, norm_below, 0)
    norm_recv[ind] = lane_sums([norm_span[k] for k in range(K - 1)] + [norm_all - norm_span[K - 1]])
    pl.semaphore_wait(barrier, 15)
    for o in range(1, N_IND):
        norm_copy(o).start()

    def send_scores(s):
        spots[...] = jnp.zeros_like(spots)

        def below(b, carry):
            q = places[24 + b]
            p = places[28 + b]
            held = []
            for t in range(TJ):
                held.append(jnp.where(t * 1024 + place < p, r[q * TJ + t], 0.0))
            for c in range(BV):
                row = rows[s, c]
                total = prefix[q, c]
                for t in range(TJ):
                    total = total + held[t] * tile(q * TJ + t, row)
                part[pl.ds(pl.multiple_of((b * BV + c) * 8, 8), 8), :] = total - spots[c]
                spots[c] = total
            return carry

        lax.fori_loop(0, K - 1, below, 0)
        for c in range(BV):
            at = ((K - 1) * BV + c) * 8
            part[at : at + 8, :] = prefix[NS, c] - spots[c]
        values = []
        for k in range(K):
            groups = []
            for a in range(BV // 8):
                total = part[pl.ds((k * BV + a * 8) * 8, 8, stride=8), :]
                for sub in range(1, 8):
                    total = total + part[pl.ds((k * BV + a * 8) * 8 + sub, 8, stride=8), :]
                groups.append(total)
            values.append(jnp.concatenate(groups, axis=0))
        ind_recv[s, ind] = jnp.concatenate([lane_sums(values), jnp.zeros((8, 128 - BV), F32)], axis=1)
        for o in range(1, N_IND):
            ind_copy(s, o).start()

    send_scores(0)

    inverse = [1.0 / jnp.full((1, BV), noise[k], F32) for k in range(K)]

    def selector(s):
        return (lax.broadcasted_iota(jnp.int32, (ROWS, BV), 0) == rows_v[pl.ds(s, 1), :]).astype(F32)

    def entry(a, b):
        return a * (a + 1) // 2 + b

    n_entries = entry(K, 0)

    for o in range(1, N_IND):
        norm_copy(o).wait_recv()
    norm_total = norm_recv[0]
    for other in range(1, N_IND):
        norm_total = norm_total + norm_recv[other]

    def factor(s, carry):
        norm = jnp.dot(norm_total, selector(s), precision=HIGHEST, preferred_element_type=F32)
        lower = [[None] * K for a in range(K)]
        scale = [None] * K
        for a in range(K):
            for b in range(a + 1):
                total = jnp.full((1, BV), prior[a, b], F32)
                if a == b:
                    total = total + norm[a : a + 1] * inverse[a]
                for m in range(b):
                    total = total - lower[a][m] * lower[b][m]
                if a == b:
                    scale[a] = 1.0 / jnp.sqrt(total)
                    lower[a][a] = scale[a]
                else:
                    lower[a][b] = total * scale[b]
                factors[s, entry(a, b) : entry(a, b) + 1, :] = lower[a][b]
        for k in range(K):
            factors[s, n_entries + k : n_entries + k + 1, :] = norm[k : k + 1]
        return carry

    lax.fori_loop(0, STEPS, factor, 0)

    def step(s, carry):
        chosen = selector(s)
        before = jnp.dot(eff[...], chosen, precision=HIGHEST, preferred_element_type=F32)
        for o in range(1, N_IND):
            ind_copy(s, o).wait_recv()
        scores = ind_recv[s, 0]
        for other in range(1, N_IND):
            scores = scores + ind_recv[s, other]
        scores = scores[:, 0:BV]

        def lower(a, b):
            return factors[s, entry(a, b) : entry(a, b) + 1, :]

        forward = []
        for a in range(K):
            norm = factors[s, n_entries + a : n_entries + a + 1, :]
            total = (scores[a : a + 1] + norm * before[a : a + 1]) * inverse[a]
            for m in range(a):
                total = total - lower(a, m) * forward[m]
            forward.append(total * lower(a, a) + gauss[s, a : a + 1, :])
        drawn = [None] * K
        for a in reversed(range(K)):
            total = forward[a]
            for m in range(a + 1, K):
                total = total - lower(m, a) * drawn[m]
            drawn[a] = total * lower(a, a)
        rest = jnp.zeros((8 - K, BV), F32)
        change = jnp.concatenate([drawn[k] - before[k : k + 1] for k in range(K)] + [rest], axis=0)
        changes[...] = change

        def splat(k, carry):
            line = changes[pl.ds(k, 1), :]
            for c in range(BV):
                table[k * BV + c] = jnp.broadcast_to(line[:, c : c + 1], (8, 128))
            return carry

        lax.fori_loop(0, K, splat, 0)
        eff[...] = eff[...] + lax.dot_general(
            change, chosen, contract_last, precision=HIGHEST, preferred_element_type=F32
        )

        def fixes(b, carry):
            q = places[24 + b]
            p = places[32 + b]
            totals = [jnp.zeros((8, 128), F32)] * TJ
            for c in range(BV):
                row = rows[s, c]
                more = table[(b + 1) * BV + c] - table[b * BV + c]
                for t in range(TJ):
                    totals[t] = totals[t] + more * tile(q * TJ + t, row)
            for t in range(TJ):
                fix[b, t] = jnp.where(t * 1024 + place >= p, totals[t], 0.0)
            return carry

        lax.fori_loop(0, K - 1, fixes, 0)

        def spread(n, carry):
            half, m = n // 8, n % 8
            o = (1 - m % 2) * 4 + far_first(m // 2)
            q = chip_at(o, 1) * 2 + core * half + (1 - core) * (1 - half)
            k = places[q]
            totals = [jnp.zeros((8, 128), F32)] * TJ
            for c in range(BV):
                row = rows[s, c]
                factor_c = table[k * BV + c]
                for t in range(TJ):
                    totals[t] = totals[t] + factor_c * tile(q * TJ + t, row)
            for b in range(K - 1):
                here = jnp.full((8, 128), places[24 + b], jnp.int32) == q
                for t in range(TJ):
                    totals[t] = totals[t] + jnp.where(here, fix[b, t], 0.0)
            mine = jnp.stack(totals)

            @pl.when(n < 8)
            def _():
                core_send[o] = mine
                core_copy(o).start()

            @pl.when(n >= 8)
            def _():
                core_copy(o).wait_recv()
                far_send[o] = mine + core_recv[o]

                @pl.when(n < 15)
                def _():
                    far_copy(o).start()

            return carry

        lax.fori_loop(0, 16, spread, 0)
        mine = far_send[0]
        for o in NEAR_FIRST:
            far_copy(o).wait_recv()
            mine = mine + far_recv[o]
        own = slice_tiles(var)
        r[own] = r[own] - mine

        @pl.when(s < STEPS - 1)
        def _():
            for o in FAR_FIRST:
                gather_copy(o).start()
            forward_copy(0).start()
            for o in NEAR_FIRST:
                gather_copy(o).wait_recv()
                forward_copy(o).start()
            for o in range(8):
                forward_copy(o).wait_recv()

            def sweep(q, carry):
                score_slice(s + 1, q)
                return carry

            lax.fori_loop(0, NS, sweep, 0)
            send_scores(s + 1)
            for o in range(8):
                forward_copy(o).wait_send()
            for o in FAR_FIRST:
                gather_copy(o).wait_send()

        for o in range(1, N_IND):
            ind_copy(s, o).wait_send()
        for o in range(8):
            core_copy(o).wait_send()
        for o in FAR_FIRST:
            far_copy(o).wait_send()
        return carry

    lax.fori_loop(0, STEPS, step, 0)
    out_r[...] = r[slice_tiles(var)]
    out_eff[...] = eff[0:K, :]
    for o in range(1, N_IND):
        norm_copy(o).wait_send()


def find_places(anc, places):
    totals = [jnp.zeros((8, 128), jnp.int32)] * (K - 1)
    for j in range(NJ):
        a = anc[j]
        totals = [t + (a < b + 1).astype(jnp.int32) for b, t in enumerate(totals)]
    begins = [jnp.sum(t) for t in totals]
    for q in range(NS):
        places[q] = sum([(begins[b] <= q * (TJ * 1024)).astype(jnp.int32) for b in range(K - 1)])
    for b in range(K - 1):
        c = jnp.minimum(lax.div(begins[b], CJ * 1024), NCH - 1)
        q = jnp.minimum(lax.div(begins[b], TJ * 1024), NS - 1)
        inside = begins[b] - q * (TJ * 1024)
        places[16 + b] = c
        places[20 + b] = begins[b] - c * (CJ * 1024)
        places[24 + b] = q
        places[28 + b] = inside
        places[32 + b] = jnp.where(inside > 0, inside, TJ * 1024)


def per_device(genotypes, residual, ancestry, effects, prior_precision, noise_var, block_index, gaussians):
    whole = pl.BlockSpec(memory_space=pltpu.VMEM)
    scalar = pl.BlockSpec(memory_space=pltpu.SMEM)
    anywhere = pl.BlockSpec(memory_space=pl.ANY)
    dma = pltpu.SemaphoreType.DMA
    places = pl.pallas_call(
        find_places,
        name="find_places",
        out_shape=jax.ShapeDtypeStruct((36,), jnp.int32),
        in_specs=[whole],
        out_specs=scalar,
    )(ancestry.reshape(NJ, 8, 128))
    new, new_effects = pl.pallas_call(
        kernel,
        name="gibbs",
        out_shape=(jax.ShapeDtypeStruct((TJ, 8, 128), F32), jax.ShapeDtypeStruct((K, ROWS), F32)),
        in_specs=[anywhere, anywhere, scalar, whole, scalar, scalar, scalar, whole, whole],
        out_specs=(whole, whole),
        scratch_shapes=[
            pltpu.VMEM((NJ * ROWS, 8, 128), F32),
            pltpu.VMEM((NBUF, ROWS, CJ * 1024), jnp.bfloat16),
            pltpu.VMEM((NJ, 8, 128), F32),
            pltpu.VMEM((8, ROWS), F32),
            pltpu.VMEM((NS + 1, BV, 8, 128), F32),
            pltpu.VMEM((NCH, ROWS, 128), F32),
            pltpu.VMEM((K * BV * 8, 128), F32),
            pltpu.VMEM((BV, 8, 128), F32),
            pltpu.VMEM((K * BV, 8, 128), F32),
            pltpu.VMEM((K - 1, TJ, 8, 128), F32),
            pltpu.VMEM((64, 128), F32),
            pltpu.VMEM((K, ROWS, 128), F32),
            pltpu.VMEM((STEPS, 24, BV), F32),
            pltpu.VMEM((8, BV), F32),
            pltpu.VMEM((8, TJ, 8, 128), F32),
            pltpu.VMEM((8, TJ, 8, 128), F32),
            pltpu.VMEM((8, TJ, 8, 128), F32),
            pltpu.VMEM((8, TJ, 8, 128), F32),
            pltpu.VMEM((N_IND, 8, 128), F32),
            pltpu.VMEM((STEPS, N_IND, 8, 128), F32),
            dma((NBUF,)),
            dma,
            dma((8,)),
            dma((8,)),
            dma((8,)),
            dma((8,)),
            dma((8,)),
            dma((8,)),
            dma((8,)),
            dma((8,)),
            dma((N_IND,)),
            dma((N_IND,)),
            dma((STEPS, N_IND)),
            dma((STEPS, N_IND)),
        ],
        compiler_params=pltpu.CompilerParams(
            vmem_limit_bytes=63 * 1024 * 1024, collective_id=0, has_side_effects=True
        ),
    )(
        genotypes,
        residual.reshape(NJ, 8, 128),
        places,
        effects,
        prior_precision,
        noise_var,
        block_index,
        block_index,
        gaussians,
    )
    return new.reshape(-1), new_effects


def solution(mesh):
    return jax.shard_map(
        per_device,
        mesh=mesh,
        in_specs=(
            P("var", "ind"),
            P("ind"),
            P("ind"),
            P(None, "var"),
            P(),
            P(),
            P(None, "var"),
            P(None, None, "var"),
        ),
        out_specs=(P(("ind", "var")), P(None, "var")),
        check_vma=False,
    )
```

```python
import functools

import jax
import jax.numpy as jnp
from jax import lax
from jax.experimental import pallas as pl
from jax.experimental.pallas import tpu as pltpu
from jax.sharding import PartitionSpec as P

MESH = pl.DeviceIdType.MESH
HIGHEST = lax.Precision.HIGHEST
F32 = jnp.float32

K = 5
ROWS = 128
BV = 32
STEPS = 3
NJ = 96
TJ = 6
NS = NJ // TJ
CJ = 3
NCH = NJ // CJ
NBUF = 6
N_IND = 8
LAG = 4
FAR_FIRST = (6, 2, 5, 7, 4, 1, 3)
NEAR_FIRST = (1, 3, 4, 5, 7, 2, 6)


def offset(m):
    half = m // 2
    return (1 - m % 2) * 4 + (2 + 3 * half + 3 * (half * (half - 1) // 2)) % 4


def kernel(
    g_hbm, r_hbm, places, eff_in, prior, noise, rows, rows_v, gauss,
    out_r, out_eff,
    wide, stage, r, eff, prefix, norm_prefix, part, table, fix,
    norm_part, norm_span, factors,
    mine_send, core_recv, far_send, far_recv, norm_recv, ind_recv,
    load_sem, in_sem, core_ss, core_rs, far_ss, far_rs, ag_ss, ag_rs, fw_ss, fw_rs, nrm_ss, nrm_rs, ind_ss, ind_rs,
):
    ind, var = lax.axis_index("ind"), lax.axis_index("var")
    core, chip = var % 2, var // 2
    x, z = chip % 4, chip // 4
    y, zh = ind % 4, ind // 4
    partner = var + 1 - 2 * core

    def chip_at(o, sign):
        return ((z + o // 4) % 2) * 4 + (x + sign * (o % 4) + 4) % 4

    def ind_at(o):
        return ((zh + o // 4) % 2) * 4 + (y + o % 4) % 4

    def slice_tiles(w):
        return pl.ds(w * TJ, TJ)

    def remote(src, dst, send, recv, to):
        return pltpu.make_async_remote_copy(
            src_ref=src, dst_ref=dst, send_sem=send, recv_sem=recv, device_id=to, device_id_type=MESH
        )

    def chunk(c, slot):
        at = pl.multiple_of(c * CJ * 1024, CJ * 1024)
        return pltpu.make_async_copy(g_hbm.at[:, pl.ds(at, CJ * 1024)], stage.at[slot], load_sem.at[slot])

    def core_copy(o):
        return remote(mine_send.at[o, 1 - core], core_recv.at[o], core_ss.at[o], core_rs.at[o], (ind, partner))

    def far_copy(o):
        return remote(
            far_send.at[o], far_recv.at[o], far_ss.at[o], far_rs.at[o], (ind, chip_at(o, 1) * 2 + core)
        )

    def gather_copy(o):
        own = slice_tiles(var)
        return remote(r.at[own], r.at[own], ag_ss.at[o], ag_rs.at[o], (ind, chip_at(o, 1) * 2 + core))

    def forward_copy(o):
        at = slice_tiles(chip_at(o, -1) * 2 + core)
        return remote(r.at[at], r.at[at], fw_ss.at[o], fw_rs.at[o], (ind, partner))

    def norm_copy(o):
        return remote(norm_recv.at[ind], norm_recv.at[ind], nrm_ss.at[o], nrm_rs.at[o], (ind_at(o), var))

    def ind_copy(s, o):
        return remote(ind_recv.at[s, ind], ind_recv.at[s, ind], ind_ss.at[s, o], ind_rs.at[s, o], (ind_at(o), var))

    r_copy = pltpu.make_async_copy(r_hbm, r, in_sem)
    r_copy.start()
    for c in range(NBUF):
        chunk(c, c).start()

    barrier = pltpu.get_barrier_semaphore()
    pl.semaphore_signal(barrier, inc=1, device_id=(ind, partner), device_id_type=MESH)
    for o in range(1, 8):
        pl.semaphore_signal(barrier, inc=1, device_id=(ind, chip_at(o, 1) * 2 + core), device_id_type=MESH)
    for o in range(1, N_IND):
        pl.semaphore_signal(barrier, inc=1, device_id=(ind_at(o), var), device_id_type=MESH)

    r_copy.wait()
    eff[...] = jnp.zeros_like(eff)
    eff[0:K, :] = eff_in[...]

    lanes = lax.broadcasted_iota(jnp.int32, (8, 128), 1)
    place = lax.broadcasted_iota(jnp.int32, (8, 128), 0) * 128 + lanes

    wide_rows = wide.reshape(NJ * ROWS * 8, 128)

    def tile(j, row):
        return wide[j * ROWS + row]

    def score_slice(s, q):
        held = [r[q * TJ + t] for t in range(TJ)]
        for c in range(BV):
            row = rows[s, c]
            total = prefix[q, c]
            for t in range(TJ):
                total = total + held[t] * tile(q * TJ + t, row)
            prefix[q + 1, c] = total

    prefix[0] = jnp.zeros_like(prefix[0])

    def load(q, norm):
        for h in range(TJ // CJ):
            c = q * (TJ // CJ) + h
            slot = lax.rem(c, NBUF)
            chunk(c, slot).wait()
            norm_prefix[c] = norm

            def widen(jj, norm):
                sums = [norm[a * 16 : (a + 1) * 16] for a in range(8)]
                for a in range(8):
                    for t in range(8):
                        at = pl.multiple_of(jj * 1024 + t * 128, 128)
                        v = stage[slot, a * 16 : (a + 1) * 16, pl.ds(at, 128)].astype(F32)
                        wide_rows[pl.ds((c * CJ + jj) * (ROWS * 8) + a * 128 + t, 16, stride=8), :] = v
                        sums[a] = sums[a] + v * v
                return jnp.concatenate(sums, axis=0)

            norm = lax.fori_loop(0, CJ, widen, norm, unroll=True)

            @pl.when(c + NBUF < NCH)
            def _():
                chunk(c + NBUF, slot).start()

        score_slice(0, q)
        return norm

    norm_all = lax.fori_loop(0, NS, load, jnp.zeros((ROWS, 128), F32))

    contract_last = (((1,), (1,)), ((), ()))

    def lane_sums(values):
        return jnp.sum(values.T, axis=0, keepdims=True)

    def message(lines):
        return jnp.concatenate(lines + [jnp.zeros((8 - len(lines), 128), F32)], axis=0)

    norm_span[K - 1] = jnp.zeros((ROWS, 128), F32)

    def norm_below(b, carry):
        c = places[16 + b]
        p = places[20 + b]
        keep = [t * 1024 + place < p for t in range(CJ)]

        def some_rows(a, carry):
            for i in range(8):
                total = jnp.zeros((8, 128), F32)
                for t in range(CJ):
                    v = tile(c * CJ + t, a * 8 + i)
                    total = total + jnp.where(keep[t], v * v, 0.0)
                norm_part[a % 4, i * 8 : (i + 1) * 8, :] = total
            at = pl.ds(pl.multiple_of(a * 8, 8), 8)
            here = norm_prefix[c, at, :]
            for sub in range(8):
                here = here + norm_part[a % 4, pl.ds(sub, 8, stride=8), :]
            norm_span[b, at, :] = here - norm_span[K - 1, at, :]
            norm_span[K - 1, at, :] = here
            return carry

        return lax.fori_loop(0, ROWS // 8, some_rows, carry, unroll=4)

    lax.fori_loop(0, K - 1, norm_below, 0)
    norm_recv[ind] = message(
        [lane_sums(norm_span[k]) for k in range(K - 1)] + [lane_sums(norm_all - norm_span[K - 1])]
    )
    pl.semaphore_wait(barrier, 15)
    for o in range(1, N_IND):
        norm_copy(o).start()

    def send_scores(s):
        slices = [places[24 + b] for b in range(K - 1)]
        held = []
        for b in range(K - 1):
            p = places[28 + b]
            held.append([jnp.where(t * 1024 + place < p, r[slices[b] * TJ + t], 0.0) for t in range(TJ)])
        for c in range(BV):
            row = rows[s, c]
            below = [jnp.zeros((8, 128), F32)]
            for b in range(K - 1):
                total = prefix[slices[b], c]
                for t in range(TJ):
                    total = total + held[b][t] * tile(slices[b] * TJ + t, row)
                below.append(total)
            below.append(prefix[NS, c])
            for k in range(K):
                part[(k * BV + c) * 8 : (k * BV + c + 1) * 8, :] = below[k + 1] - below[k]
        groups = []
        for k in range(K):
            for a in range(BV // 8):
                total = part[pl.ds((k * BV + a * 8) * 8, 8, stride=8), :]
                for sub in range(1, 8):
                    total = total + part[pl.ds((k * BV + a * 8) * 8 + sub, 8, stride=8), :]
                groups.append(total)
        most = lane_sums(jnp.concatenate(groups[: 128 // 8], axis=0))
        last = lane_sums(jnp.concatenate(groups[128 // 8 :], axis=0))
        ind_recv[s, ind] = message([most, jnp.concatenate([last, jnp.zeros((1, 128 - BV), F32)], axis=1)])
        for o in range(1, N_IND):
            ind_copy(s, o).start()

    send_scores(0)

    inverse = [1.0 / jnp.full((1, BV), noise[k], F32) for k in range(K)]

    def selector(s):
        return (lax.broadcasted_iota(jnp.int32, (ROWS, BV), 0) == rows_v[pl.ds(s, 1), :]).astype(F32)

    def entry(a, b):
        return a * (a + 1) // 2 + b

    n_entries = entry(K, 0)

    for o in range(1, N_IND):
        norm_copy(o).wait_recv()
    norm_total = norm_recv[0]
    for other in range(1, N_IND):
        norm_total = norm_total + norm_recv[other]

    def factor(s, carry):
        norm = jnp.dot(norm_total, selector(s), precision=HIGHEST, preferred_element_type=F32)
        lower = [[None] * K for a in range(K)]
        scale = [None] * K
        for a in range(K):
            for b in range(a + 1):
                total = jnp.full((1, BV), prior[a, b], F32)
                if a == b:
                    total = total + norm[a : a + 1] * inverse[a]
                for m in range(b):
                    total = total - lower[a][m] * lower[b][m]
                if a == b:
                    scale[a] = 1.0 / jnp.sqrt(total)
                    lower[a][a] = scale[a]
                else:
                    lower[a][b] = total * scale[b]
                factors[s, entry(a, b) : entry(a, b) + 1, :] = lower[a][b]
        for k in range(K):
            factors[s, n_entries + k : n_entries + k + 1, :] = norm[k : k + 1]
        return carry

    lax.fori_loop(0, STEPS, factor, 0)

    def step(s, carry):
        chosen = selector(s)
        before = jnp.dot(eff[...], chosen, precision=HIGHEST, preferred_element_type=F32)
        for o in range(1, N_IND):
            ind_copy(s, o).wait_recv()
        scores = ind_recv[s, 0]
        for other in range(1, N_IND):
            scores = scores + ind_recv[s, other]
        scores = [scores[0:1, k * BV : (k + 1) * BV] for k in range(K - 1)] + [scores[1:2, 0:BV]]

        def lower(a, b):
            return factors[s, entry(a, b) : entry(a, b) + 1, :]

        forward = []
        for a in range(K):
            norm = factors[s, n_entries + a : n_entries + a + 1, :]
            total = (scores[a] + norm * before[a : a + 1]) * inverse[a]
            for m in range(a):
                total = total - lower(a, m) * forward[m]
            forward.append(total * lower(a, a) + gauss[a, pl.ds(s, 1), :])
        drawn = [None] * K
        for a in reversed(range(K)):
            total = forward[a]
            for m in range(a + 1, K):
                total = total - lower(m, a) * drawn[m]
            drawn[a] = total * lower(a, a)
        rest = jnp.zeros((8 - K, BV), F32)
        change = jnp.concatenate([drawn[k] - before[k : k + 1] for k in range(K)] + [rest], axis=0)

        for k in range(K):
            for c in range(BV):
                table[k * BV + c] = jnp.broadcast_to(change[k : k + 1, c : c + 1], (8, 128))
        eff[...] = eff[...] + lax.dot_general(
            change, chosen, contract_last, precision=HIGHEST, preferred_element_type=F32
        )

        slices = [places[24 + b] for b in range(K - 1)]
        totals = [[jnp.zeros((8, 128), F32)] * TJ for b in range(K - 1)]
        for c in range(BV):
            row = rows[s, c]
            low = table[c]
            for b in range(K - 1):
                high = table[(b + 1) * BV + c]
                for t in range(TJ):
                    totals[b][t] = totals[b][t] + (high - low) * tile(slices[b] * TJ + t, row)
                low = high
        for b in range(K - 1):
            p = places[32 + b]
            for t in range(TJ):
                fix[b, t] = jnp.where(t * 1024 + place >= p, totals[b][t], 0.0)

        def spread(n, carry):
            @pl.when(n < 8)
            def _():
                o = offset(n)
                q = chip_at(o, 1) * 2
                both = [[jnp.zeros((8, 128), F32)] * TJ for half in range(2)]
                first = [places[q + half] * BV for half in range(2)]
                for c in range(BV):
                    row = rows[s, c]
                    for half in range(2):
                        factor_c = table[first[half] + c]
                        for t in range(TJ):
                            both[half][t] = both[half][t] + factor_c * tile((q + half) * TJ + t, row)
                for b in range(K - 1):
                    at = jnp.full((8, 128), places[24 + b], jnp.int32)
                    for t in range(TJ):
                        more = fix[b, t]
                        for half in range(2):
                            both[half][t] = both[half][t] + jnp.where(at == q + half, more, 0.0)
                for half in range(2):
                    mine_send[o, half] = jnp.stack(both[half])
                core_copy(o).start()

            @pl.when(n >= LAG)
            def _():
                o = offset(n - LAG)
                core_copy(o).wait_recv()
                far_send[o] = mine_send[o, core] + core_recv[o]

                @pl.when(n < LAG + 7)
                def _():
                    far_copy(o).start()

            return carry

        lax.fori_loop(0, 8 + LAG, spread, 0)
        mine = far_send[0]
        for o in NEAR_FIRST:
            far_copy(o).wait_recv()
            mine = mine + far_recv[o]
        own = slice_tiles(var)
        r[own] = r[own] - mine

        @pl.when(s < STEPS - 1)
        def _():
            for o in FAR_FIRST:
                gather_copy(o).start()

            forward_copy(0).start()
            for o in NEAR_FIRST:
                gather_copy(o).wait_recv()
                forward_copy(o).start()
            for o in range(8):
                forward_copy(o).wait_recv()

            def sweep(q, carry):
                score_slice(s + 1, q)
                return carry

            lax.fori_loop(0, NS, sweep, 0)
            send_scores(s + 1)
            for o in range(8):
                forward_copy(o).wait_send()
            for o in FAR_FIRST:
                gather_copy(o).wait_send()

        for o in range(1, N_IND):
            ind_copy(s, o).wait_send()
        for o in range(8):
            core_copy(o).wait_send()
        for o in FAR_FIRST:
            far_copy(o).wait_send()
        return carry

    lax.fori_loop(0, STEPS, step, 0)
    out_r[...] = r[slice_tiles(var)]
    out_eff[...] = eff[0:K, :]
    for o in range(1, N_IND):
        norm_copy(o).wait_send()


def find_places(anc, places):
    totals = [jnp.zeros((8, 128), jnp.int32)] * (K - 1)
    for j in range(NJ):
        a = anc[j]
        totals = [t + (a < b + 1).astype(jnp.int32) for b, t in enumerate(totals)]
    begins = [jnp.sum(t) for t in totals]
    for q in range(NS):
        places[q] = sum([(begins[b] <= q * (TJ * 1024)).astype(jnp.int32) for b in range(K - 1)])
    for b in range(K - 1):
        c = jnp.minimum(lax.div(begins[b], CJ * 1024), NCH - 1)
        q = jnp.minimum(lax.div(begins[b], TJ * 1024), NS - 1)
        inside = begins[b] - q * (TJ * 1024)
        places[16 + b] = c
        places[20 + b] = begins[b] - c * (CJ * 1024)
        places[24 + b] = q
        places[28 + b] = inside
        places[32 + b] = jnp.where(inside > 0, inside, TJ * 1024)


def hand_over(new, new_effects, out_r, out_eff):
    out_r[...] = new[...]
    out_eff[...] = new_effects[...]


def per_device(genotypes, residual, ancestry, effects, prior_precision, noise_var, block_index, gaussians):
    whole = pl.BlockSpec(memory_space=pltpu.VMEM)
    scalar = pl.BlockSpec(memory_space=pltpu.SMEM)
    anywhere = pl.BlockSpec(memory_space=pl.ANY)
    dma = pltpu.SemaphoreType.DMA
    places = pl.pallas_call(
        find_places,
        name="find_places",
        out_shape=jax.ShapeDtypeStruct((36,), jnp.int32),
        in_specs=[whole],
        out_specs=scalar,
    )(ancestry.reshape(NJ, 8, 128))
    new, new_effects = pl.pallas_call(
        kernel,
        name="gibbs",
        out_shape=(jax.ShapeDtypeStruct((TJ, 8, 128), F32), jax.ShapeDtypeStruct((K, ROWS), F32)),
        in_specs=[anywhere, anywhere, scalar, whole, scalar, scalar, scalar, whole, whole],
        out_specs=(whole, whole),
        scratch_shapes=[
            pltpu.VMEM((NJ * ROWS, 8, 128), F32),
            pltpu.VMEM((NBUF, ROWS, CJ * 1024), jnp.bfloat16),
            pltpu.VMEM((NJ, 8, 128), F32),
            pltpu.VMEM((8, ROWS), F32),
            pltpu.VMEM((NS + 1, BV, 8, 128), F32),
            pltpu.VMEM((NCH, ROWS, 128), F32),
            pltpu.VMEM((K * BV * 8, 128), F32),
            pltpu.VMEM((K * BV, 8, 128), F32),
            pltpu.VMEM((K - 1, TJ, 8, 128), F32),
            pltpu.VMEM((4, 64, 128), F32),
            pltpu.VMEM((K, ROWS, 128), F32),
            pltpu.VMEM((STEPS, 24, BV), F32),
            pltpu.VMEM((8, 2, TJ, 8, 128), F32),
            pltpu.VMEM((8, TJ, 8, 128), F32),
            pltpu.VMEM((8, TJ, 8, 128), F32),
            pltpu.VMEM((8, TJ, 8, 128), F32),
            pltpu.VMEM((N_IND, 8, 128), F32),
            pltpu.VMEM((STEPS, N_IND, 8, 128), F32),
            dma((NBUF,)),
            dma,
            dma((8,)),
            dma((8,)),
            dma((8,)),
            dma((8,)),
            dma((8,)),
            dma((8,)),
            dma((8,)),
            dma((8,)),
            dma((N_IND,)),
            dma((N_IND,)),
            dma((STEPS, N_IND)),
            dma((STEPS, N_IND)),
        ],
        compiler_params=pltpu.CompilerParams(
            vmem_limit_bytes=63 * 1024 * 1024, collective_id=0, has_side_effects=True
        ),
    )(
        genotypes,
        residual.reshape(NJ, 8, 128),
        places,
        effects,
        prior_precision,
        noise_var,
        block_index,
        block_index,
        gaussians.transpose(1, 0, 2),
    )
    new, new_effects = pl.pallas_call(
        hand_over,
        name="hand_over",
        out_shape=(jax.ShapeDtypeStruct((TJ, 8, 128), F32), jax.ShapeDtypeStruct((K, ROWS), F32)),
        in_specs=[whole, whole],
        out_specs=(whole, whole),
    )(new, new_effects)
    return new.reshape(-1), new_effects


def solution(mesh):
    return jax.shard_map(
        per_device,
        mesh=mesh,
        in_specs=(
            P("var", "ind"),
            P("ind"),
            P("ind"),
            P(None, "var"),
            P(),
            P(),
            P(None, "var"),
            P(None, None, "var"),
        ),
        out_specs=(P(("ind", "var")), P(None, "var")),
        check_vma=False,
    )
```

```python
import functools

import jax
import jax.numpy as jnp
from jax import lax
from jax.experimental import pallas as pl
from jax.experimental.pallas import tpu as pltpu
from jax.sharding import PartitionSpec as P

MESH = pl.DeviceIdType.MESH
HIGHEST = lax.Precision.HIGHEST
F32 = jnp.float32

K = 5
ROWS = 128
BV = 32
STEPS = 3
NJ = 96
TJ = 6
NS = NJ // TJ
CJ = 3
NCH = NJ // CJ
NBUF = 6
N_IND = 8
FAR_FIRST = (6, 2, 5, 7, 4, 1, 3)
NEAR_FIRST = (1, 3, 4, 5, 7, 2, 6)


def offset(m):
    half = m // 2
    return (1 - m % 2) * 4 + (2 + 3 * half + 3 * (half * (half - 1) // 2)) % 4


def kernel(
    g_hbm, r_hbm, anc_hbm, eff_in, prior, noise, rows, rows_v, gauss,
    out_r, out_eff,
    wide, stage, r, anc, eff, prefix, norm_prefix, part, table, fix,
    norm_part, norm_span, factors,
    mine_send, core_recv, far_send, far_recv, norm_recv, ind_recv,
    load_sem, in_sem, core_ss, core_rs, far_ss, far_rs, ag_ss, ag_rs, fw_ss, fw_rs, nrm_ss, nrm_rs, ind_ss, ind_rs,
):
    ind, var = lax.axis_index("ind"), lax.axis_index("var")
    core, chip = var % 2, var // 2
    x, z = chip % 4, chip // 4
    y, zh = ind % 4, ind // 4
    partner = var + 1 - 2 * core

    def chip_at(o, sign):
        return ((z + o // 4) % 2) * 4 + (x + sign * (o % 4) + 4) % 4

    def ind_at(o):
        return ((zh + o // 4) % 2) * 4 + (y + o % 4) % 4

    def slice_tiles(w):
        return pl.ds(w * TJ, TJ)

    def remote(src, dst, send, recv, to):
        return pltpu.make_async_remote_copy(
            src_ref=src, dst_ref=dst, send_sem=send, recv_sem=recv, device_id=to, device_id_type=MESH
        )

    def chunk(c, slot):
        at = pl.multiple_of(c * CJ * 1024, CJ * 1024)
        return pltpu.make_async_copy(g_hbm.at[:, pl.ds(at, CJ * 1024)], stage.at[slot], load_sem.at[slot])

    def core_copy(o):
        return remote(mine_send.at[o, 1 - core], core_recv.at[o], core_ss.at[o], core_rs.at[o], (ind, partner))

    def far_copy(o):
        return remote(
            far_send.at[o], far_recv.at[o], far_ss.at[o], far_rs.at[o], (ind, chip_at(o, 1) * 2 + core)
        )

    def gather_copy(o):
        own = slice_tiles(var)
        return remote(r.at[own], r.at[own], ag_ss.at[o], ag_rs.at[o], (ind, chip_at(o, 1) * 2 + core))

    def forward_copy(o):
        at = slice_tiles(chip_at(o, -1) * 2 + core)
        return remote(r.at[at], r.at[at], fw_ss.at[o], fw_rs.at[o], (ind, partner))

    def norm_copy(o):
        return remote(norm_recv.at[ind], norm_recv.at[ind], nrm_ss.at[o], nrm_rs.at[o], (ind_at(o), var))

    def ind_copy(s, o):
        return remote(ind_recv.at[s, ind], ind_recv.at[s, ind], ind_ss.at[s, o], ind_rs.at[s, o], (ind_at(o), var))

    anc_copy = pltpu.make_async_copy(anc_hbm, anc, in_sem.at[0])
    r_copy = pltpu.make_async_copy(r_hbm, r, in_sem.at[1])
    anc_copy.start()
    r_copy.start()
    for c in range(NBUF):
        chunk(c, c).start()

    barrier = pltpu.get_barrier_semaphore()
    pl.semaphore_signal(barrier, inc=1, device_id=(ind, partner), device_id_type=MESH)
    for o in range(1, 8):
        pl.semaphore_signal(barrier, inc=1, device_id=(ind, chip_at(o, 1) * 2 + core), device_id_type=MESH)
    for o in range(1, N_IND):
        pl.semaphore_signal(barrier, inc=1, device_id=(ind_at(o), var), device_id_type=MESH)

    anc_copy.wait()

    def count(group, totals):
        for i in range(8):
            a = anc[group * 8 + i]
            totals = tuple(t + (a < b + 1).astype(jnp.int32) for b, t in enumerate(totals))
        return totals

    totals = lax.fori_loop(0, NJ // 8, count, (jnp.zeros((8, 128), jnp.int32),) * (K - 1))
    begins = [jnp.sum(t) for t in totals]
    chunk_of = [jnp.minimum(lax.div(p, CJ * 1024), NCH - 1) for p in begins]
    slice_of = [jnp.minimum(lax.div(p, TJ * 1024), NS - 1) for p in begins]
    r_copy.wait()
    eff[...] = jnp.zeros_like(eff)
    eff[0:K, :] = eff_in[...]

    lanes = lax.broadcasted_iota(jnp.int32, (8, 128), 1)
    place = lax.broadcasted_iota(jnp.int32, (8, 128), 0) * 128 + lanes

    wide_rows = wide.reshape(NJ * ROWS * 8, 128)

    def tile(j, row):
        return wide[j * ROWS + row]

    def score_slice(s, q):
        held = [r[q * TJ + t] for t in range(TJ)]
        for c in range(BV):
            row = rows[s, c]
            total = prefix[q, c]
            for t in range(TJ):
                total = total + held[t] * tile(q * TJ + t, row)
            prefix[q + 1, c] = total

    prefix[0] = jnp.zeros_like(prefix[0])

    def load(q, norm):
        for h in range(TJ // CJ):
            c = q * (TJ // CJ) + h
            slot = lax.rem(c, NBUF)
            chunk(c, slot).wait()
            norm_prefix[c] = norm

            def widen(jj, norm):
                sums = [norm[a * 16 : (a + 1) * 16] for a in range(8)]
                for a in range(8):
                    for t in range(8):
                        at = pl.multiple_of(jj * 1024 + t * 128, 128)
                        v = stage[slot, a * 16 : (a + 1) * 16, pl.ds(at, 128)].astype(F32)
                        wide_rows[pl.ds((c * CJ + jj) * (ROWS * 8) + a * 128 + t, 16, stride=8), :] = v
                        sums[a] = sums[a] + v * v
                return jnp.concatenate(sums, axis=0)

            norm = lax.fori_loop(0, CJ, widen, norm, unroll=True)

            @pl.when(c + NBUF < NCH)
            def _():
                chunk(c + NBUF, slot).start()

        score_slice(0, q)
        return norm

    norm_all = lax.fori_loop(0, NS, load, jnp.zeros((ROWS, 128), F32))

    contract_last = (((1,), (1,)), ((), ()))

    def lane_sums(values):
        return jnp.sum(values.T, axis=0, keepdims=True)

    def message(lines):
        return jnp.concatenate(lines + [jnp.zeros((8 - len(lines), 128), F32)], axis=0)

    norm_span[K - 1] = jnp.zeros((ROWS, 128), F32)

    def norm_below(b):
        c = chunk_of[b]
        p = begins[b] - c * (CJ * 1024)
        keep = [t * 1024 + place < p for t in range(CJ)]

        def some_rows(a, carry):
            for i in range(8):
                total = jnp.zeros((8, 128), F32)
                for t in range(CJ):
                    v = tile(c * CJ + t, a * 8 + i)
                    total = total + jnp.where(keep[t], v * v, 0.0)
                norm_part[a % 4, i * 8 : (i + 1) * 8, :] = total
            at = pl.ds(pl.multiple_of(a * 8, 8), 8)
            here = norm_prefix[c, at, :]
            for sub in range(8):
                here = here + norm_part[a % 4, pl.ds(sub, 8, stride=8), :]
            norm_span[b, at, :] = here - norm_span[K - 1, at, :]
            norm_span[K - 1, at, :] = here
            return carry

        lax.fori_loop(0, ROWS // 8, some_rows, 0, unroll=4)

    for b in range(K - 1):
        norm_below(b)
    norm_recv[ind] = message(
        [lane_sums(norm_span[k]) for k in range(K - 1)] + [lane_sums(norm_all - norm_span[K - 1])]
    )
    pl.semaphore_wait(barrier, 15)
    for o in range(1, N_IND):
        norm_copy(o).start()

    def send_scores(s):
        slices = slice_of
        held = []
        for b in range(K - 1):
            p = begins[b] - slices[b] * (TJ * 1024)
            held.append([jnp.where(t * 1024 + place < p, r[slices[b] * TJ + t], 0.0) for t in range(TJ)])
        for c in range(BV):
            row = rows[s, c]
            below = [jnp.zeros((8, 128), F32)]
            for b in range(K - 1):
                total = prefix[slices[b], c]
                for t in range(TJ):
                    total = total + held[b][t] * tile(slices[b] * TJ + t, row)
                below.append(total)
            below.append(prefix[NS, c])
            for k in range(K):
                part[(k * BV + c) * 8 : (k * BV + c + 1) * 8, :] = below[k + 1] - below[k]
        groups = []
        for k in range(K):
            for a in range(BV // 8):
                total = part[pl.ds((k * BV + a * 8) * 8, 8, stride=8), :]
                for sub in range(1, 8):
                    total = total + part[pl.ds((k * BV + a * 8) * 8 + sub, 8, stride=8), :]
                groups.append(total)
        most = lane_sums(jnp.concatenate(groups[: 128 // 8], axis=0))
        last = lane_sums(jnp.concatenate(groups[128 // 8 :], axis=0))
        ind_recv[s, ind] = message([most, jnp.concatenate([last, jnp.zeros((1, 128 - BV), F32)], axis=1)])
        for o in range(1, N_IND):
            ind_copy(s, o).start()

    send_scores(0)

    inverse = [1.0 / jnp.full((1, BV), noise[k], F32) for k in range(K)]

    def selector(s):
        return (lax.broadcasted_iota(jnp.int32, (ROWS, BV), 0) == rows_v[pl.ds(s, 1), :]).astype(F32)

    def entry(a, b):
        return a * (a + 1) // 2 + b

    n_entries = entry(K, 0)

    for o in range(1, N_IND):
        norm_copy(o).wait_recv()
    norm_total = norm_recv[0]
    for other in range(1, N_IND):
        norm_total = norm_total + norm_recv[other]

    def factor(s, carry):
        norm = jnp.dot(norm_total, selector(s), precision=HIGHEST, preferred_element_type=F32)
        lower = [[None] * K for a in range(K)]
        scale = [None] * K
        for a in range(K):
            for b in range(a + 1):
                total = jnp.full((1, BV), prior[a, b], F32)
                if a == b:
                    total = total + norm[a : a + 1] * inverse[a]
                for m in range(b):
                    total = total - lower[a][m] * lower[b][m]
                if a == b:
                    scale[a] = 1.0 / jnp.sqrt(total)
                    lower[a][a] = scale[a]
                else:
                    lower[a][b] = total * scale[b]
                factors[s, entry(a, b) : entry(a, b) + 1, :] = lower[a][b]
        for k in range(K):
            factors[s, n_entries + k : n_entries + k + 1, :] = norm[k : k + 1]
        return carry

    lax.fori_loop(0, STEPS, factor, 0)

    def step(s, carry):
        chosen = selector(s)
        before = jnp.dot(eff[...], chosen, precision=HIGHEST, preferred_element_type=F32)
        for o in range(1, N_IND):
            ind_copy(s, o).wait_recv()
        scores = ind_recv[s, 0]
        for other in range(1, N_IND):
            scores = scores + ind_recv[s, other]
        scores = [scores[0:1, k * BV : (k + 1) * BV] for k in range(K - 1)] + [scores[1:2, 0:BV]]

        def lower(a, b):
            return factors[s, entry(a, b) : entry(a, b) + 1, :]

        forward = []
        for a in range(K):
            norm = factors[s, n_entries + a : n_entries + a + 1, :]
            total = (scores[a] + norm * before[a : a + 1]) * inverse[a]
            for m in range(a):
                total = total - lower(a, m) * forward[m]
            forward.append(total * lower(a, a) + gauss[a, pl.ds(s, 1), :])
        drawn = [None] * K
        for a in reversed(range(K)):
            total = forward[a]
            for m in range(a + 1, K):
                total = total - lower(m, a) * drawn[m]
            drawn[a] = total * lower(a, a)
        rest = jnp.zeros((8 - K, BV), F32)
        change = jnp.concatenate([drawn[k] - before[k : k + 1] for k in range(K)] + [rest], axis=0)

        for k in range(K):
            for c in range(BV):
                table[k * BV + c] = jnp.broadcast_to(change[k : k + 1, c : c + 1], (8, 128))
        eff[...] = eff[...] + lax.dot_general(
            change, chosen, contract_last, precision=HIGHEST, preferred_element_type=F32
        )

        slices = slice_of
        totals = [[jnp.zeros((8, 128), F32)] * TJ for b in range(K - 1)]
        for c in range(BV):
            row = rows[s, c]
            low = table[c]
            for b in range(K - 1):
                high = table[(b + 1) * BV + c]
                for t in range(TJ):
                    totals[b][t] = totals[b][t] + (high - low) * tile(slices[b] * TJ + t, row)
                low = high
        for b in range(K - 1):
            p = jnp.full((8, 128), begins[b] - slices[b] * (TJ * 1024), jnp.int32)
            for t in range(TJ):
                fix[b, t] = jnp.where((t * 1024 + place >= p) & (p > 0), totals[b][t], 0.0)

        def spread(n, carry):
            half, m = n // 8, n % 8
            o = offset(m)
            q = chip_at(o, 1) * 2 + core * half + (1 - core) * (1 - half)
            k = sum([(p <= q * (TJ * 1024)).astype(jnp.int32) for p in begins])
            totals = [jnp.zeros((8, 128), F32)] * TJ
            for c in range(BV):
                row = rows[s, c]
                factor_c = table[k * BV + c]
                for t in range(TJ):
                    totals[t] = totals[t] + factor_c * tile(q * TJ + t, row)
            for b in range(K - 1):
                here = jnp.full((8, 128), slice_of[b], jnp.int32) == q
                for t in range(TJ):
                    totals[t] = totals[t] + jnp.where(here, fix[b, t], 0.0)
            mine = jnp.stack(totals)

            @pl.when(n < 8)
            def _():
                mine_send[o, 1 - core] = mine
                core_copy(o).start()

            @pl.when(n >= 8)
            def _():
                core_copy(o).wait_recv()
                far_send[o] = mine + core_recv[o]

                @pl.when(n < 15)
                def _():
                    far_copy(o).start()

            return carry

        lax.fori_loop(0, 16, spread, 0)
        mine = far_send[0]
        for o in NEAR_FIRST:
            far_copy(o).wait_recv()
            mine = mine + far_recv[o]
        own = slice_tiles(var)
        r[own] = r[own] - mine

        @pl.when(s < STEPS - 1)
        def _():
            for o in FAR_FIRST:
                gather_copy(o).start()

            forward_copy(0).start()
            for o in NEAR_FIRST:
                gather_copy(o).wait_recv()
                forward_copy(o).start()
            for o in range(8):
                forward_copy(o).wait_recv()

            def sweep(q, carry):
                score_slice(s + 1, q)
                return carry

            lax.fori_loop(0, NS, sweep, 0)
            send_scores(s + 1)
            for o in range(8):
                forward_copy(o).wait_send()
            for o in FAR_FIRST:
                gather_copy(o).wait_send()

        for o in range(1, N_IND):
            ind_copy(s, o).wait_send()
        for o in range(8):
            core_copy(o).wait_send()
        for o in FAR_FIRST:
            far_copy(o).wait_send()
        return carry

    lax.fori_loop(0, STEPS, step, 0)
    out_r[...] = r[slice_tiles(var)]
    out_eff[...] = eff[0:K, :]
    for o in range(1, N_IND):
        norm_copy(o).wait_send()


def hand_over(new, new_effects, out_r, out_eff):
    out_r[...] = new[...]
    out_eff[...] = new_effects[...]


def per_device(genotypes, residual, ancestry, effects, prior_precision, noise_var, block_index, gaussians):
    whole = pl.BlockSpec(memory_space=pltpu.VMEM)
    scalar = pl.BlockSpec(memory_space=pltpu.SMEM)
    anywhere = pl.BlockSpec(memory_space=pl.ANY)
    dma = pltpu.SemaphoreType.DMA
    new, new_effects = pl.pallas_call(
        kernel,
        name="gibbs",
        out_shape=(jax.ShapeDtypeStruct((TJ, 8, 128), F32), jax.ShapeDtypeStruct((K, ROWS), F32)),
        in_specs=[anywhere, anywhere, anywhere, whole, scalar, scalar, scalar, whole, whole],
        out_specs=(whole, whole),
        scratch_shapes=[
            pltpu.VMEM((NJ * ROWS, 8, 128), F32),
            pltpu.VMEM((NBUF, ROWS, CJ * 1024), jnp.bfloat16),
            pltpu.VMEM((NJ, 8, 128), F32),
            pltpu.VMEM((NJ, 8, 128), jnp.int32),
            pltpu.VMEM((8, ROWS), F32),
            pltpu.VMEM((NS + 1, BV, 8, 128), F32),
            pltpu.VMEM((NCH, ROWS, 128), F32),
            pltpu.VMEM((K * BV * 8, 128), F32),
            pltpu.VMEM((K * BV, 8, 128), F32),
            pltpu.VMEM((K - 1, TJ, 8, 128), F32),
            pltpu.VMEM((4, 64, 128), F32),
            pltpu.VMEM((K, ROWS, 128), F32),
            pltpu.VMEM((STEPS, 24, BV), F32),
            pltpu.VMEM((8, 2, TJ, 8, 128), F32),
            pltpu.VMEM((8, TJ, 8, 128), F32),
            pltpu.VMEM((8, TJ, 8, 128), F32),
            pltpu.VMEM((8, TJ, 8, 128), F32),
            pltpu.VMEM((N_IND, 8, 128), F32),
            pltpu.VMEM((STEPS, N_IND, 8, 128), F32),
            dma((NBUF,)),
            dma((2,)),
            dma((8,)),
            dma((8,)),
            dma((8,)),
            dma((8,)),
            dma((8,)),
            dma((8,)),
            dma((8,)),
            dma((8,)),
            dma((N_IND,)),
            dma((N_IND,)),
            dma((STEPS, N_IND)),
            dma((STEPS, N_IND)),
        ],
        compiler_params=pltpu.CompilerParams(
            vmem_limit_bytes=63 * 1024 * 1024, collective_id=0, has_side_effects=True
        ),
    )(
        genotypes,
        residual.reshape(NJ, 8, 128),
        ancestry.reshape(NJ, 8, 128),
        effects,
        prior_precision,
        noise_var,
        block_index,
        block_index,
        gaussians.transpose(1, 0, 2),
    )
    new, new_effects = pl.pallas_call(
        hand_over,
        name="hand_over",
        out_shape=(jax.ShapeDtypeStruct((TJ, 8, 128), F32), jax.ShapeDtypeStruct((K, ROWS), F32)),
        in_specs=[whole, whole],
        out_specs=(whole, whole),
    )(new, new_effects)
    return new.reshape(-1), new_effects


def solution(mesh):
    return jax.shard_map(
        per_device,
        mesh=mesh,
        in_specs=(
            P("var", "ind"),
            P("ind"),
            P("ind"),
            P(None, "var"),
            P(),
            P(),
            P(None, "var"),
            P(None, None, "var"),
        ),
        out_specs=(P(("ind", "var")), P(None, "var")),
        check_vma=False,
    )
```

```python
import functools

import jax
import jax.numpy as jnp
from jax import lax
from jax.experimental import pallas as pl
from jax.experimental.pallas import tpu as pltpu
from jax.sharding import PartitionSpec as P

MESH = pl.DeviceIdType.MESH
HIGHEST = lax.Precision.HIGHEST
F32 = jnp.float32

K = 5
ROWS = 128
BV = 32
STEPS = 3
NJ = 96
TJ = 6
NS = NJ // TJ
CJ = 3
NCH = NJ // CJ
NBUF = 6
N_IND = 8
FAR_FIRST = (6, 2, 5, 7, 4, 1, 3)
NEAR_FIRST = (1, 3, 4, 5, 7, 2, 6)
IND_FAR_FIRST = (6, 5, 7, 2, 4, 1, 3)


def offset(m):
    half = m // 2
    return (1 - m % 2) * 4 + (2 + 3 * half + 3 * (half * (half - 1) // 2)) % 4


def kernel(
    g_hbm, r_hbm, anc_hbm, eff_in, prior, noise, rows, rows_v, gauss,
    out_r, out_eff,
    wide, stage, r, anc, eff, prefix, norm_prefix, part, table, fix,
    norm_part, norm_span, factors,
    mine_send, core_recv, far_send, far_recv, norm_recv, ind_recv,
    load_sem, in_sem, core_ss, core_rs, far_ss, far_rs, ag_ss, ag_rs, fw_ss, fw_rs, nrm_ss, nrm_rs, ind_ss, ind_rs,
):
    ind, var = lax.axis_index("ind"), lax.axis_index("var")
    core, chip = var % 2, var // 2
    x, z = chip % 4, chip // 4
    y, zh = ind % 4, ind // 4
    partner = var + 1 - 2 * core

    def chip_at(o, sign):
        return ((z + o // 4) % 2) * 4 + (x + sign * (o % 4) + 4) % 4

    def ind_at(o):
        return ((zh + o // 4) % 2) * 4 + (y + o % 4) % 4

    def slice_tiles(w):
        return pl.ds(w * TJ, TJ)

    def remote(src, dst, send, recv, to):
        return pltpu.make_async_remote_copy(
            src_ref=src, dst_ref=dst, send_sem=send, recv_sem=recv, device_id=to, device_id_type=MESH
        )

    def chunk(c, slot):
        at = pl.multiple_of(c * CJ * 1024, CJ * 1024)
        return pltpu.make_async_copy(g_hbm.at[:, pl.ds(at, CJ * 1024)], stage.at[slot], load_sem.at[slot])

    def core_copy(o):
        return remote(mine_send.at[o, 1 - core], core_recv.at[o], core_ss.at[o], core_rs.at[o], (ind, partner))

    def far_copy(o):
        return remote(
            far_send.at[o], far_recv.at[o], far_ss.at[o], far_rs.at[o], (ind, chip_at(o, 1) * 2 + core)
        )

    def gather_copy(o):
        own = slice_tiles(var)
        return remote(r.at[own], r.at[own], ag_ss.at[o], ag_rs.at[o], (ind, chip_at(o, 1) * 2 + core))

    def forward_copy(o):
        at = slice_tiles(chip_at(o, -1) * 2 + core)
        return remote(r.at[at], r.at[at], fw_ss.at[o], fw_rs.at[o], (ind, partner))

    def norm_copy(o):
        return remote(norm_recv.at[ind], norm_recv.at[ind], nrm_ss.at[o], nrm_rs.at[o], (ind_at(o), var))

    def ind_copy(s, o):
        return remote(ind_recv.at[s, ind], ind_recv.at[s, ind], ind_ss.at[s, o], ind_rs.at[s, o], (ind_at(o), var))

    anc_copy = pltpu.make_async_copy(anc_hbm, anc, in_sem.at[0])
    r_copy = pltpu.make_async_copy(r_hbm, r, in_sem.at[1])
    anc_copy.start()
    r_copy.start()
    for c in range(NBUF):
        chunk(c, c).start()

    barrier = pltpu.get_barrier_semaphore()
    pl.semaphore_signal(barrier, inc=1, device_id=(ind, partner), device_id_type=MESH)
    for o in range(1, 8):
        pl.semaphore_signal(barrier, inc=1, device_id=(ind, chip_at(o, 1) * 2 + core), device_id_type=MESH)
    for o in range(1, N_IND):
        pl.semaphore_signal(barrier, inc=1, device_id=(ind_at(o), var), device_id_type=MESH)

    anc_copy.wait()

    def count(group, totals):
        for i in range(8):
            a = anc[group * 8 + i]
            totals = tuple(t + (a < b + 1).astype(jnp.int32) for b, t in enumerate(totals))
        return totals

    totals = lax.fori_loop(0, NJ // 8, count, (jnp.zeros((8, 128), jnp.int32),) * (K - 1))
    begins = [jnp.sum(t) for t in totals]
    chunk_of = [jnp.minimum(lax.div(p, CJ * 1024), NCH - 1) for p in begins]
    slice_of = [jnp.minimum(lax.div(p, TJ * 1024), NS - 1) for p in begins]
    r_copy.wait()
    eff[...] = jnp.zeros_like(eff)
    eff[0:K, :] = eff_in[...]

    lanes = lax.broadcasted_iota(jnp.int32, (8, 128), 1)
    place = lax.broadcasted_iota(jnp.int32, (8, 128), 0) * 128 + lanes

    wide_rows = wide.reshape(NJ * ROWS * 8, 128)

    def tile(j, row):
        return wide[j * ROWS + row]

    def score_slice(s, q):
        held = [r[q * TJ + t] for t in range(TJ)]
        for c in range(BV):
            row = rows[s, c]
            total = prefix[q, c]
            for t in range(TJ):
                total = total + held[t] * tile(q * TJ + t, row)
            prefix[q + 1, c] = total

    prefix[0] = jnp.zeros_like(prefix[0])

    def load(q, norm):
        for h in range(TJ // CJ):
            c = q * (TJ // CJ) + h
            slot = lax.rem(c, NBUF)
            chunk(c, slot).wait()
            norm_prefix[c] = norm

            def widen(jj, norm):
                sums = [norm[a * 16 : (a + 1) * 16] for a in range(8)]
                for a in range(8):
                    for t in range(8):
                        at = pl.multiple_of(jj * 1024 + t * 128, 128)
                        v = stage[slot, a * 16 : (a + 1) * 16, pl.ds(at, 128)].astype(F32)
                        wide_rows[pl.ds((c * CJ + jj) * (ROWS * 8) + a * 128 + t, 16, stride=8), :] = v
                        sums[a] = sums[a] + v * v
                return jnp.concatenate(sums, axis=0)

            norm = lax.fori_loop(0, CJ, widen, norm, unroll=True)

            @pl.when(c + NBUF < NCH)
            def _():
                chunk(c + NBUF, slot).start()

        score_slice(0, q)
        return norm

    norm_all = lax.fori_loop(0, NS, load, jnp.zeros((ROWS, 128), F32))

    contract_last = (((1,), (1,)), ((), ()))

    def lane_sums(values):
        return jnp.sum(values.T, axis=0, keepdims=True)

    def message(lines):
        return jnp.concatenate(lines + [jnp.zeros((8 - len(lines), 128), F32)], axis=0)

    norm_span[K - 1] = jnp.zeros((ROWS, 128), F32)

    def norm_below(b):
        c = chunk_of[b]
        p = begins[b] - c * (CJ * 1024)
        keep = [t * 1024 + place < p for t in range(CJ)]

        def some_rows(a, carry):
            for i in range(8):
                total = jnp.zeros((8, 128), F32)
                for t in range(CJ):
                    v = tile(c * CJ + t, a * 8 + i)
                    total = total + jnp.where(keep[t], v * v, 0.0)
                norm_part[a % 4, i * 8 : (i + 1) * 8, :] = total
            at = pl.ds(pl.multiple_of(a * 8, 8), 8)
            here = norm_prefix[c, at, :]
            for sub in range(8):
                here = here + norm_part[a % 4, pl.ds(sub, 8, stride=8), :]
            norm_span[b, at, :] = here - norm_span[K - 1, at, :]
            norm_span[K - 1, at, :] = here
            return carry

        lax.fori_loop(0, ROWS // 8, some_rows, 0, unroll=4)

    for b in range(K - 1):
        norm_below(b)
    norm_recv[ind] = message(
        [lane_sums(norm_span[k]) for k in range(K - 1)] + [lane_sums(norm_all - norm_span[K - 1])]
    )
    pl.semaphore_wait(barrier, 15)
    for o in IND_FAR_FIRST:
        norm_copy(o).start()

    def send_scores(s):
        slices = slice_of
        held = []
        for b in range(K - 1):
            p = begins[b] - slices[b] * (TJ * 1024)
            held.append([jnp.where(t * 1024 + place < p, r[slices[b] * TJ + t], 0.0) for t in range(TJ)])
        for c in range(BV):
            row = rows[s, c]
            below = [jnp.zeros((8, 128), F32)]
            for b in range(K - 1):
                total = prefix[slices[b], c]
                for t in range(TJ):
                    total = total + held[b][t] * tile(slices[b] * TJ + t, row)
                below.append(total)
            below.append(prefix[NS, c])
            for k in range(K):
                part[(k * BV + c) * 8 : (k * BV + c + 1) * 8, :] = below[k + 1] - below[k]
        groups = []
        for k in range(K):
            for a in range(BV // 8):
                total = part[pl.ds((k * BV + a * 8) * 8, 8, stride=8), :]
                for sub in range(1, 8):
                    total = total + part[pl.ds((k * BV + a * 8) * 8 + sub, 8, stride=8), :]
                groups.append(total)
        most = lane_sums(jnp.concatenate(groups[: 128 // 8], axis=0))
        last = lane_sums(jnp.concatenate(groups[128 // 8 :], axis=0))
        ind_recv[s, ind] = message([most, jnp.concatenate([last, jnp.zeros((1, 128 - BV), F32)], axis=1)])
        for o in IND_FAR_FIRST:
            ind_copy(s, o).start()

    send_scores(0)

    inverse = [1.0 / jnp.full((1, BV), noise[k], F32) for k in range(K)]

    def selector(s):
        return (lax.broadcasted_iota(jnp.int32, (ROWS, BV), 0) == rows_v[pl.ds(s, 1), :]).astype(F32)

    def entry(a, b):
        return a * (a + 1) // 2 + b

    n_entries = entry(K, 0)

    for o in range(1, N_IND):
        norm_copy(o).wait_recv()
    norm_total = norm_recv[0]
    for other in range(1, N_IND):
        norm_total = norm_total + norm_recv[other]

    def factor(s, carry):
        norm = jnp.dot(norm_total, selector(s), precision=HIGHEST, preferred_element_type=F32)
        lower = [[None] * K for a in range(K)]
        scale = [None] * K
        for a in range(K):
            for b in range(a + 1):
                total = jnp.full((1, BV), prior[a, b], F32)
                if a == b:
                    total = total + norm[a : a + 1] * inverse[a]
                for m in range(b):
                    total = total - lower[a][m] * lower[b][m]
                if a == b:
                    scale[a] = 1.0 / jnp.sqrt(total)
                    lower[a][a] = scale[a]
                else:
                    lower[a][b] = total * scale[b]
                factors[s, entry(a, b) : entry(a, b) + 1, :] = lower[a][b]
        for k in range(K):
            factors[s, n_entries + k : n_entries + k + 1, :] = norm[k : k + 1]
        return carry

    lax.fori_loop(0, STEPS, factor, 0)

    def step(s, carry):
        chosen = selector(s)
        before = jnp.dot(eff[...], chosen, precision=HIGHEST, preferred_element_type=F32)
        for o in range(1, N_IND):
            ind_copy(s, o).wait_recv()
        scores = ind_recv[s, 0]
        for other in range(1, N_IND):
            scores = scores + ind_recv[s, other]
        scores = [scores[0:1, k * BV : (k + 1) * BV] for k in range(K - 1)] + [scores[1:2, 0:BV]]

        def lower(a, b):
            return factors[s, entry(a, b) : entry(a, b) + 1, :]

        forward = []
        for a in range(K):
            norm = factors[s, n_entries + a : n_entries + a + 1, :]
            total = (scores[a] + norm * before[a : a + 1]) * inverse[a]
            for m in range(a):
                total = total - lower(a, m) * forward[m]
            forward.append(total * lower(a, a) + gauss[a, pl.ds(s, 1), :])
        drawn = [None] * K
        for a in reversed(range(K)):
            total = forward[a]
            for m in range(a + 1, K):
                total = total - lower(m, a) * drawn[m]
            drawn[a] = total * lower(a, a)
        rest = jnp.zeros((8 - K, BV), F32)
        change = jnp.concatenate([drawn[k] - before[k : k + 1] for k in range(K)] + [rest], axis=0)

        for k in range(K):
            for c in range(BV):
                table[k * BV + c] = jnp.broadcast_to(change[k : k + 1, c : c + 1], (8, 128))
        eff[...] = eff[...] + lax.dot_general(
            change, chosen, contract_last, precision=HIGHEST, preferred_element_type=F32
        )

        slices = slice_of
        totals = [[jnp.zeros((8, 128), F32)] * TJ for b in range(K - 1)]
        for c in range(BV):
            row = rows[s, c]
            low = table[c]
            for b in range(K - 1):
                high = table[(b + 1) * BV + c]
                for t in range(TJ):
                    totals[b][t] = totals[b][t] + (high - low) * tile(slices[b] * TJ + t, row)
                low = high
        for b in range(K - 1):
            p = jnp.full((8, 128), begins[b] - slices[b] * (TJ * 1024), jnp.int32)
            for t in range(TJ):
                fix[b, t] = jnp.where((t * 1024 + place >= p) & (p > 0), totals[b][t], 0.0)

        def spread(n, carry):
            half, m = n // 8, n % 8
            o = offset(m)
            q = chip_at(o, 1) * 2 + core * half + (1 - core) * (1 - half)
            k = sum([(p <= q * (TJ * 1024)).astype(jnp.int32) for p in begins])
            totals = [jnp.zeros((8, 128), F32)] * TJ
            for c in range(BV):
                row = rows[s, c]
                factor_c = table[k * BV + c]
                for t in range(TJ):
                    totals[t] = totals[t] + factor_c * tile(q * TJ + t, row)
            for b in range(K - 1):
                here = jnp.full((8, 128), slice_of[b], jnp.int32) == q
                for t in range(TJ):
                    totals[t] = totals[t] + jnp.where(here, fix[b, t], 0.0)
            mine = jnp.stack(totals)

            @pl.when(n < 8)
            def _():
                mine_send[o, 1 - core] = mine
                core_copy(o).start()

            @pl.when(n >= 8)
            def _():
                core_copy(o).wait_recv()
                far_send[o] = mine + core_recv[o]

                @pl.when(n < 15)
                def _():
                    far_copy(o).start()

            return carry

        lax.fori_loop(0, 16, spread, 0)
        mine = far_send[0]
        for o in NEAR_FIRST:
            far_copy(o).wait_recv()
            mine = mine + far_recv[o]
        own = slice_tiles(var)
        r[own] = r[own] - mine

        @pl.when(s < STEPS - 1)
        def _():
            for o in FAR_FIRST:
                gather_copy(o).start()

            forward_copy(0).start()
            for o in NEAR_FIRST:
                gather_copy(o).wait_recv()
                forward_copy(o).start()
            for o in range(8):
                forward_copy(o).wait_recv()

            def sweep(q, carry):
                score_slice(s + 1, q)
                return carry

            lax.fori_loop(0, NS, sweep, 0)
            send_scores(s + 1)
            for o in range(8):
                forward_copy(o).wait_send()
            for o in FAR_FIRST:
                gather_copy(o).wait_send()

        for o in range(1, N_IND):
            ind_copy(s, o).wait_send()
        for o in range(8):
            core_copy(o).wait_send()
        for o in FAR_FIRST:
            far_copy(o).wait_send()
        return carry

    lax.fori_loop(0, STEPS, step, 0)
    out_r[...] = r[slice_tiles(var)]
    out_eff[...] = eff[0:K, :]
    for o in range(1, N_IND):
        norm_copy(o).wait_send()


def hand_over(new, new_effects, out_r, out_eff):
    out_r[...] = new[...]
    out_eff[...] = new_effects[...]


def per_device(genotypes, residual, ancestry, effects, prior_precision, noise_var, block_index, gaussians):
    whole = pl.BlockSpec(memory_space=pltpu.VMEM)
    scalar = pl.BlockSpec(memory_space=pltpu.SMEM)
    anywhere = pl.BlockSpec(memory_space=pl.ANY)
    dma = pltpu.SemaphoreType.DMA
    new, new_effects = pl.pallas_call(
        kernel,
        name="gibbs",
        out_shape=(jax.ShapeDtypeStruct((TJ, 8, 128), F32), jax.ShapeDtypeStruct((K, ROWS), F32)),
        in_specs=[anywhere, anywhere, anywhere, whole, scalar, scalar, scalar, whole, whole],
        out_specs=(whole, whole),
        scratch_shapes=[
            pltpu.VMEM((NJ * ROWS, 8, 128), F32),
            pltpu.VMEM((NBUF, ROWS, CJ * 1024), jnp.bfloat16),
            pltpu.VMEM((NJ, 8, 128), F32),
            pltpu.VMEM((NJ, 8, 128), jnp.int32),
            pltpu.VMEM((8, ROWS), F32),
            pltpu.VMEM((NS + 1, BV, 8, 128), F32),
            pltpu.VMEM((NCH, ROWS, 128), F32),
            pltpu.VMEM((K * BV * 8, 128), F32),
            pltpu.VMEM((K * BV, 8, 128), F32),
            pltpu.VMEM((K - 1, TJ, 8, 128), F32),
            pltpu.VMEM((4, 64, 128), F32),
            pltpu.VMEM((K, ROWS, 128), F32),
            pltpu.VMEM((STEPS, 24, BV), F32),
            pltpu.VMEM((8, 2, TJ, 8, 128), F32),
            pltpu.VMEM((8, TJ, 8, 128), F32),
            pltpu.VMEM((8, TJ, 8, 128), F32),
            pltpu.VMEM((8, TJ, 8, 128), F32),
            pltpu.VMEM((N_IND, 8, 128), F32),
            pltpu.VMEM((STEPS, N_IND, 8, 128), F32),
            dma((NBUF,)),
            dma((2,)),
            dma((8,)),
            dma((8,)),
            dma((8,)),
            dma((8,)),
            dma((8,)),
            dma((8,)),
            dma((8,)),
            dma((8,)),
            dma((N_IND,)),
            dma((N_IND,)),
            dma((STEPS, N_IND)),
            dma((STEPS, N_IND)),
        ],
        compiler_params=pltpu.CompilerParams(
            vmem_limit_bytes=63 * 1024 * 1024, collective_id=0, has_side_effects=True
        ),
    )(
        genotypes,
        residual.reshape(NJ, 8, 128),
        ancestry.reshape(NJ, 8, 128),
        effects,
        prior_precision,
        noise_var,
        block_index,
        block_index,
        gaussians.transpose(1, 0, 2),
    )
    new, new_effects = pl.pallas_call(
        hand_over,
        name="hand_over",
        out_shape=(jax.ShapeDtypeStruct((TJ, 8, 128), F32), jax.ShapeDtypeStruct((K, ROWS), F32)),
        in_specs=[whole, whole],
        out_specs=(whole, whole),
    )(new, new_effects)
    return new.reshape(-1), new_effects


def solution(mesh):
    return jax.shard_map(
        per_device,
        mesh=mesh,
        in_specs=(
            P("var", "ind"),
            P("ind"),
            P("ind"),
            P(None, "var"),
            P(),
            P(),
            P(None, "var"),
            P(None, None, "var"),
        ),
        out_specs=(P(("ind", "var")), P(None, "var")),
        check_vma=False,
    )
```
